256 devices in a mesh: batch: 32 (over x_hi, z, core), head: 8 (over y, x_lo).
Axes of the slice: x: 4 (x_hi: 2, x_lo: 2; x = x_hi * 2 + x_lo), y: 4, z: 8, core: 2. Of those that a mesh axis runs over, the one named last changes fastest.
Arguments:
- ssm_values: bfloat16 [64, 256, 16384], P('batch', None, 'head'), may hold values from -6 to 6
- ssm_gate: bfloat16 [64, 256, 16384], P('batch', None, 'head'), may hold values from -6 to 6
- ssm_keys: bfloat16 [64, 256, 2048], P('batch', None, 'head'), may hold values from -6 to 6
- ssm_queries: bfloat16 [64, 256, 2048], P('batch', None, 'head'), may hold values from -0.375 to 0.375
- step_sizes: float32 [64, 256, 256], P('batch', None, 'head'), as said below
- decay_rates: float32 [256], P('head'), as said below
- skip_weights: float32 [256], P('head'), may hold values from 0.25 to 1.75
- norm_gain: float32 [16384], P('head'), may hold values from 0.5 to 1.5
- att_queries: bfloat16 [64, 256, 8192], P('batch', None, 'head'), may hold values from -64 to 64
- new_keyvals: bfloat16 [64, 256, 2048], P('batch', None, 'head'), may hold values from -32 to 32
- page_pool: bfloat16 [1024, 1024, 256], P('batch', 'head'), may hold values from -6 to 6
- page_owner: int32 [64, 32, 1], P('batch'), may hold values from 0 to 31; in each aligned block of 64 rows (0 to 63, 64 to 127, ..., all dimensions but the last counted through in order) at most 4 rows name the same one
- page_slot: int32 [64, 32], P('batch'), may hold values from 0 to 31
- new_lengths: int32 [64], P('batch'), may hold values from 64 to 256, as said below
- cached_lengths: int32 [64], P('batch'), may hold values from 128 to 2048, as said below
Outputs:
- mixer_out: bfloat16 [64, 256, 16384], P('batch', None, 'head')
- attention_out: bfloat16 [64, 256, 8192], P('batch', None, 'head')
The draws below stay inside these ranges and needn't reach their ends.
Inputs may be any that keep to these rules, and one draw needn't show every extreme that they name: `page_owner`: within the rows of one device's requests, no owner is named more than 4 times; in some device's rows one owner is named exactly 4 times. `new_lengths`: some request has 256 new tokens. `cached_lengths`: some request has 2048 cached tokens. `step_sizes`: Positive. `decay_rates`: Positive.
All inputs are finite; a program needn't handle non-finite values.
Results may differ from the reference program's by a relative error of at most 0.0049.
Values may be sent and summed in bfloat16 or wider, within the bound.
No kernel may reach another device: no remote copies, remote signals or barrier semaphores. Data moves between devices by JAX's collectives and lax.ppermute only.
A program may use at most 128 MiB of HBM per device.

```python
import math
import jax
import jax.numpy as jnp
import numpy as np
from jax import lax

SSM_HEADS = 256
HEAD_P = 64
STATE = 256
GROUPS = 8
Q_HEADS = 64
KV_HEADS = 8
HEAD_DIM = 128
PAGE = 128
STATE_PAGES = 16
CAP = 4
REQ_DEV = 2
NEW = 256
PREFIX_PAGES = 16
PROWS = 4
ROWS = 1024
PPR = 32
POOL_DEV = 32
POOL_ALL = 1024
REQUESTS = 64
N_BATCH = 32


def draw_att_queries(key, part):
    key = jax.random.fold_in(key, 1)
    base = jax.random.normal(jax.random.fold_in(key, 1), (REQUESTS, NEW, Q_HEADS, HEAD_DIM), jnp.float32)
    base = jnp.clip(base, -6.0, 6.0)
    return base.reshape(REQUESTS, NEW, Q_HEADS * HEAD_DIM).astype(jnp.bfloat16)


def draw_new_keyvals(key, part):
    key = jax.random.fold_in(key, 4)
    base = jax.random.normal(key, (REQUESTS, NEW, KV_HEADS, 2 * HEAD_DIM), jnp.float32)
    base = jnp.clip(base, -6.0, 6.0)
    return base.reshape(REQUESTS, NEW, KV_HEADS * 2 * HEAD_DIM).astype(jnp.bfloat16)


def draw_step_sizes(key, part):
    key = jax.random.fold_in(key, 5)
    array_shape = (REQUESTS, NEW, SSM_HEADS)
    coarse_estimate = jax.random.uniform(jax.random.fold_in(key, 1), array_shape, jnp.float32, 0.5, 2.0) / NEW
    places = jax.random.randint(jax.random.fold_in(key, 2), (REQUESTS, 2), 0, NEW)
    spiky_traffic = jnp.any(jnp.arange(NEW)[None, :, None] == places[:, None, :], axis=-1)
    sudden_spike = jax.random.uniform(jax.random.fold_in(key, 3), array_shape, jnp.float32, 0.5, 1.2)
    return jnp.where(spiky_traffic[:, :, None], sudden_spike, coarse_estimate)


def draw_decay_rates(key, part):
    key = jax.random.fold_in(key, 6)
    slow = jnp.exp(jax.random.uniform(jax.random.fold_in(key, 1), (SSM_HEADS,), jnp.float32, jnp.log(0.25), jnp.log(0.6)))
    fast = jnp.exp(jax.random.uniform(jax.random.fold_in(key, 2), (SSM_HEADS,), jnp.float32, jnp.log(NEW / 60.0), jnp.log(NEW / 30.0)))
    share = 0.5
    keeps = jax.random.uniform(jax.random.fold_in(key, 3), (SSM_HEADS,), jnp.float32) < share
    return jnp.where(keeps, slow, fast)


def draw_new_lengths(key, part):
    key = jax.random.fold_in(key, 7)
    lengths = jax.random.randint(jax.random.fold_in(key, 1), (REQUESTS,), NEW // 4, NEW + 1)
    fullest = jax.random.randint(jax.random.fold_in(key, 2), (), 0, REQUESTS)
    return lengths.at[fullest].set(NEW)


def draw_cached_lengths(key, part):
    key = jax.random.fold_in(key, 8)
    lengths = jax.random.randint(jax.random.fold_in(key, 1), (REQUESTS,), PAGE, PREFIX_PAGES * PAGE + 1)
    fullest = jax.random.randint(jax.random.fold_in(key, 2), (), 0, REQUESTS)
    return lengths.at[fullest].set(PREFIX_PAGES * PAGE)


def plant(values, rng, smallest, high):
    spot = [jax.random.randint(jax.random.fold_in(rng, axis), (), 0, length) for axis, length in enumerate(values.shape)]
    widest = values.shape.index(max(values.shape))
    next_to = spot[:widest] + [(spot[widest] + 1) % values.shape[widest]] + spot[widest + 1:]
    return values.at[tuple(spot)].set(smallest).at[tuple(next_to)].set(high)


def block_levels(rng, shape, pieces, least, top_value):
    factor_of, own = 1.0, jax.random.fold_in(rng, 6)
    for dim, shards_of in pieces:
        steps = jnp.exp(jax.random.uniform(jax.random.fold_in(own, dim), (shards_of,), jnp.float32, least / len(pieces), top_value / len(pieces)))
        factor_of = factor_of * jnp.repeat(steps, shape[dim] // shards_of).reshape([-1 if axis == dim else 1 for axis in range(len(shape))])
    return factor_of


def deal_out(own_key, own, number, rows, count, top, most, lean):
    sequence = jax.random.permutation(own_key, count)
    packed, common = portions_of(count, rows * top, most, lean, True), portions_of(count, rows * top, most, lean, False)
    places = jnp.arange(count)

    def named(sizes, offset_by):
        used = int((sizes > 0).sum())
        fixed = max(1, used // 4)
        passed = fixed + (places - fixed + offset_by * (used - fixed)) % max(1, count - fixed)
        return jnp.zeros((count,), jnp.int32).at[sequence[jnp.where(places < fixed, places, passed)]].set(jnp.asarray(sizes, jnp.int32))

    sizes = jnp.where(number % 4 == 0, named(packed, number // 4), named(common, number - number // 4 - 1))
    mixed = jax.random.permutation(jax.random.fold_in(own, 3), count)
    source_of, receiver = mixed[0:count // 2 * 2:2], mixed[1:count // 2 * 2:2]
    slack = jnp.minimum(sizes[source_of] - 1, most - sizes[receiver]) // 2
    slack = jnp.where((source_of == sequence[0]) | (receiver == sequence[0]) | (sizes[receiver] == 0), 0, jnp.maximum(slack, 0))
    passed = jax.random.randint(jax.random.fold_in(own, 4), (count // 2,), 0, 1 << 20) % (slack + 1)
    sizes = sizes.at[source_of].add(-passed).at[receiver].add(passed)
    labels = jnp.searchsorted(jnp.cumsum(sizes), jnp.arange(rows * top), side="right").astype(jnp.int32)
    listing = labels.reshape(top, rows).T
    listing = listing[jax.random.permutation(jax.random.fold_in(own, 1), rows)]
    offset_by = jax.random.randint(jax.random.fold_in(own, 2), (rows, 1), 0, top)
    return jnp.take_along_axis(listing, (jnp.arange(top)[None, :] + offset_by) % top, axis=1)


def portions_of(amount, total, reach, slope, full):
    weights = [(1 << 20) // math.isqrt(rank ** slope) + 1 for rank in range(1, amount + 1)]
    largest = reach if full else min(reach, max(-(-total // amount), total * weights[0] // sum(weights)))
    least = 1 if total - largest >= amount - 1 else 0
    holding, rest = [largest] + [least] * (amount - 1), total - largest - least * (amount - 1)
    while rest > 0:
        free = [i for i in range(1, amount) if holding[i] < largest] or [i for i in range(1, amount) if holding[i] < reach]
        pool, left = sum([weights[i] for i in free]), rest
        for i in free:
            more = min(reach - holding[i], max(1, left * weights[i] // pool), rest)
            holding[i] = holding[i] + more
            rest = rest - more
    return np.array(holding)


def centred(key, dims, deviation, limit, pieces=(), kind=jnp.bfloat16):
    drawn = deviation * jax.random.normal(key, dims, jnp.float32)
    if pieces:
        drawn = drawn * block_levels(key, dims, pieces, -0.22, 0.18)
    return jnp.clip(drawn, -limit, limit).astype(kind)


def setup_inputs(seed: int = 0) -> dict:
    streams_of = jax.random.split(jax.random.key(seed), 16)
    ssm_values = centred(streams_of[0], (REQUESTS, NEW, SSM_HEADS * HEAD_P), 1.0, 6.0, ((0, 32), (2, 8)))
    ssm_gate = centred(streams_of[1], (REQUESTS, NEW, SSM_HEADS * HEAD_P), 1.0, 6.0, ((0, 32), (2, 8)))
    ssm_keys = centred(streams_of[2], (REQUESTS, NEW, GROUPS * STATE), 1.0, 6.0, ((0, 32), (2, 8)))
    ssm_queries = centred(streams_of[3], (REQUESTS, NEW, GROUPS * STATE), STATE ** -0.5, 0.375, ((0, 32), (2, 8)))
    step_sizes = draw_step_sizes(jax.random.fold_in(streams_of[15], 71), 0)
    decay_rates = draw_decay_rates(jax.random.fold_in(streams_of[15], 71), 0)
    skip_weights = jnp.clip(1.0 + 0.15 * jax.random.normal(streams_of[6], (SSM_HEADS,), jnp.float32), 0.25, 1.75)
    norm_gain = jnp.clip(1.0 + 0.1 * jax.random.normal(streams_of[7], (SSM_HEADS * HEAD_P,), jnp.float32), 0.5, 1.5)
    att_queries = draw_att_queries(jax.random.fold_in(streams_of[15], 71), 0)
    new_keyvals = draw_new_keyvals(jax.random.fold_in(streams_of[15], 71), 0)
    page_pool = centred(streams_of[10], (POOL_ALL, ROWS, STATE), 1.0, 6.0, ((0, 32), (1, 8)))
    page_owner_keys = jax.random.split(jax.random.fold_in(streams_of[11], 1), REQUESTS * PPR // (REQ_DEV * PPR))
    page_owner_turns = jax.random.permutation(jax.random.fold_in(streams_of[11], 3), REQUESTS * PPR // (REQ_DEV * PPR))
    page_owner = jax.vmap(lambda own, number: deal_out(jax.random.fold_in(streams_of[11], 2), own, number, REQ_DEV * PPR, N_BATCH, 1, CAP, 2))(page_owner_keys, page_owner_turns).reshape((REQUESTS, PPR, 1))
    page_slot = plant(jax.random.randint(streams_of[12], (REQUESTS, PPR), 0, POOL_DEV), jax.random.fold_in(streams_of[12], 1), 0, POOL_DEV - 1).astype(jnp.int32)
    new_lengths = draw_new_lengths(jax.random.fold_in(streams_of[15], 71), 0)
    cached_lengths = draw_cached_lengths(jax.random.fold_in(streams_of[15], 71), 0)
    return dict(ssm_values=ssm_values, ssm_gate=ssm_gate, ssm_keys=ssm_keys, ssm_queries=ssm_queries, step_sizes=step_sizes, decay_rates=decay_rates, skip_weights=skip_weights, norm_gain=norm_gain, att_queries=att_queries, new_keyvals=new_keyvals, page_pool=page_pool, page_owner=page_owner, page_slot=page_slot, new_lengths=new_lengths, cached_lengths=cached_lengths)


def mamba_block(values, gate_rows, key_rows, query_rows, step_rows, rate_rows, skip_rows, gain_rows, cached_state, length):
    new_count = values.shape[0]
    head_count = rate_rows.shape[0]
    group_count = key_rows.shape[1] // STATE
    per_group = head_count // group_count
    decay_sum = jnp.cumsum(step_rows * rate_rows[None, :], axis=0)
    keys_group = key_rows.reshape(new_count, group_count, STATE).astype(jnp.float32)
    queries_group = query_rows.reshape(new_count, group_count, STATE).astype(jnp.float32)
    inner_prod = jnp.einsum('tgn,sgn->gts', queries_group, keys_group)
    inner_prod = jnp.repeat(inner_prod, per_group, axis=0)
    positions = jnp.arange(new_count, dtype=jnp.int32)
    causal = positions[:, None] >= positions[None, :]
    lagged = decay_sum.T
    spread = jnp.where(causal[None], lagged[:, None, :] - lagged[:, :, None], 0.0)
    weights = jnp.where(causal[None], jnp.exp(spread), 0.0) * inner_prod * step_rows.T[:, None, :]
    weights = weights.astype(jnp.bfloat16)
    per_head = values.reshape(new_count, head_count, HEAD_P).astype(jnp.float32)
    fresh_part = jnp.einsum('hts,shp->thp', weights.astype(jnp.float32), per_head)
    grouped_state = cached_state.reshape(group_count, per_group, HEAD_P, STATE).astype(jnp.float32)
    carried = jnp.einsum('tgn,gkpn->tgkp', queries_group, grouped_state)
    carried = carried.reshape(new_count, head_count, HEAD_P) * jnp.exp(-decay_sum)[:, :, None]
    mixed_rows = carried + fresh_part + skip_rows[None, :, None] * per_head
    gated_rows = mixed_rows * jax.nn.silu(gate_rows.reshape(new_count, head_count, HEAD_P).astype(jnp.float32))
    gated_rows = gated_rows.reshape(new_count, group_count, per_group * HEAD_P)
    mean_square = lax.optimization_barrier(jnp.mean(gated_rows * gated_rows, axis=-1, keepdims=True))
    normed = gated_rows * lax.rsqrt(mean_square + 1e-05) * gain_rows.reshape(group_count, per_group * HEAD_P)
    normed = jnp.where(positions[:, None, None] < length, normed, 0.0)
    return normed.astype(jnp.bfloat16).reshape(new_count, head_count * HEAD_P)

def attend(queries, fresh_kv, cached_pages, length, cached):
    new_count = queries.shape[0]
    kv_count = fresh_kv.shape[1] // (2 * HEAD_DIM)
    q_group = queries.shape[1] // (HEAD_DIM * kv_count)
    page_count = cached_pages.shape[0]
    previous_rows = cached_pages.reshape(page_count, kv_count, PAGE, 2 * HEAD_DIM).transpose(1, 0, 2, 3)
    previous_rows = previous_rows.reshape(kv_count, page_count * PAGE, 2 * HEAD_DIM)
    new_rows = fresh_kv.reshape(new_count, kv_count, 2 * HEAD_DIM).transpose(1, 0, 2)
    keyvals = jnp.concatenate([previous_rows, new_rows], axis=1).astype(jnp.float32)
    grouped_heads = queries.reshape(new_count, kv_count, q_group, HEAD_DIM).astype(jnp.float32)
    scores = jnp.einsum('tkgd,ksd->kgts', grouped_heads, keyvals[:, :, :HEAD_DIM]) * HEAD_DIM ** (-0.5)
    positions = jnp.arange(new_count, dtype=jnp.int32)
    old_seen = jnp.broadcast_to(jnp.arange(page_count * PAGE, dtype=jnp.int32)[None, :] < cached, (new_count, page_count * PAGE))
    new_seen = positions[None, :] <= positions[:, None]
    visible = jnp.concatenate([old_seen, new_seen], axis=1)
    scores = jnp.where(visible, scores, -jnp.inf)
    row_max = lax.optimization_barrier(jnp.max(scores, axis=-1, keepdims=True))
    raised = jnp.exp(scores - row_max)
    probabilities = (raised / lax.optimization_barrier(jnp.sum(raised, axis=-1, keepdims=True))).astype(jnp.bfloat16)
    output = jnp.einsum('kgts,ksd->tkgd', probabilities.astype(jnp.float32), keyvals[:, :, HEAD_DIM:])
    output = jnp.where(positions[:, None, None, None] < length, output, 0.0)
    return output.astype(jnp.bfloat16).reshape(new_count, kv_count * q_group * HEAD_DIM)

def reference(ssm_values, ssm_gate, ssm_keys, ssm_queries, step_sizes, decay_rates, skip_weights, norm_gain, att_queries, new_keyvals, page_pool, page_owner, page_slot, new_lengths, cached_lengths):

    def one_request(request):
        page_index = (page_owner[request, :, 0] * POOL_DEV + page_slot[request]).astype(jnp.int32)
        request_pages = page_pool[page_index]
        cached_state = request_pages[PREFIX_PAGES:].reshape(STATE_PAGES, SSM_HEADS, PROWS, STATE)
        cached_state = cached_state.transpose(1, 0, 2, 3).reshape(SSM_HEADS, HEAD_P, STATE)
        mixer_part = mamba_block(ssm_values[request], ssm_gate[request], ssm_keys[request], ssm_queries[request], step_sizes[request], decay_rates, skip_weights, norm_gain, cached_state, new_lengths[request])
        attention = attend(att_queries[request], new_keyvals[request], request_pages[:PREFIX_PAGES], new_lengths[request], cached_lengths[request])
        return (mixer_part, attention)
    mixer_out, attention_out = lax.map(one_request, jnp.arange(REQUESTS, dtype=jnp.int32))
    return (mixer_out, attention_out)
```

```python
import functools

import jax
import jax.numpy as jnp
from jax import lax
from jax.experimental import pallas as pl
from jax.experimental.pallas import tpu as pltpu
from jax.sharding import PartitionSpec as P

HEAD_P = 64
STATE = 256
HEAD_DIM = 128
PAGE = 128
STATE_PAGES = 16
CAP = 4
BLOCK_PAGES = 4
GROUP_HEADS = 4
NEG = float("-inf")
SCORE_SCALE = HEAD_DIM**-0.5 * 1.4426950408889634
LOG2E = 1.4426950408889634
NT = (((1,), (1,)), ((), ()))
VMEM_BYTES = 48 * 1024 * 1024


def fresh_kernel(v_ref, k_ref, q_ref, dsc_ref, dsr_ref, dtr_ref, skip_ref, out_ref, inner_ref):
    new_count = v_ref.shape[1]

    @pl.when(pl.program_id(1) == 0)
    def _():
        inner_ref[...] = lax.dot_general(
            q_ref[0], k_ref[0], NT, preferred_element_type=jnp.float32
        )

    inner = inner_ref[...]
    shape = (new_count, new_count)
    causal = lax.broadcasted_iota(jnp.int32, shape, 0) >= lax.broadcasted_iota(jnp.int32, shape, 1)
    lane = lax.broadcasted_iota(jnp.int32, (new_count, 128), 1)
    for pair in range(GROUP_HEADS // 2):
        cols = slice(pair * 128, pair * 128 + 128)
        pair_values = v_ref[0, :, cols]
        parts = []
        for half in range(2):
            h = pair * 2 + half
            gap = dsr_ref[0, 0, h : h + 1, :] - dsc_ref[0, 0, :, h : h + 1]
            decay = jnp.exp2(jnp.where(causal, gap * LOG2E, NEG))
            weights = (decay * inner * dtr_ref[0, 0, h : h + 1, :]).astype(jnp.bfloat16)
            parts.append(jnp.dot(weights, pair_values, preferred_element_type=jnp.float32))
        fresh = jnp.where(lane < HEAD_P, parts[0], parts[1])
        out_ref[0, :, cols] = fresh + skip_ref[0, :, cols] * pair_values.astype(jnp.float32)


def fresh_part(values, keys, queries, ds_cols, ds_rows, dt_rows, skip_cols):
    req, new_count, width = values.shape
    block = GROUP_HEADS * HEAD_P
    groups = width // block
    return pl.pallas_call(
        fresh_kernel,
        grid=(req, groups),
        out_shape=jax.ShapeDtypeStruct(values.shape, jnp.float32),
        in_specs=[
            pl.BlockSpec((1, new_count, block), lambda r, g: (r, 0, g)),
            pl.BlockSpec((1, new_count, STATE), lambda r, g: (r, 0, 0)),
            pl.BlockSpec((1, new_count, STATE), lambda r, g: (r, 0, 0)),
            pl.BlockSpec((1, 1, new_count, GROUP_HEADS), lambda r, g: (r, g, 0, 0)),
            pl.BlockSpec((1, 1, GROUP_HEADS, new_count), lambda r, g: (r, g, 0, 0)),
            pl.BlockSpec((1, 1, GROUP_HEADS, new_count), lambda r, g: (r, g, 0, 0)),
            pl.BlockSpec((1, 1, block), lambda r, g: (0, 0, g)),
        ],
        out_specs=pl.BlockSpec((1, new_count, block), lambda r, g: (r, 0, g)),
        scratch_shapes=[pltpu.VMEM((new_count, new_count), jnp.float32)],
        compiler_params=pltpu.CompilerParams(
            dimension_semantics=("arbitrary", "arbitrary"), vmem_limit_bytes=VMEM_BYTES
        ),
        cost_estimate=pl.CostEstimate(
            flops=2 * req * 32 * 256 * 256 * 256, bytes_accessed=8 << 20, transcendentals=4 << 20
        ),
        name="ssm_fresh",
    )(values, keys, queries, ds_cols, ds_rows, dt_rows, skip_cols)


def mixer_kernel(
    index_ref, len_ref, fresh_ref, gate_ref, q_ref, dsc_ref, gain_ref, pages_ref, out_ref, states, gated_ref, sems
):
    r = pl.program_id(0)
    req = states.shape[0]
    new_count = q_ref.shape[1]
    groups = dsc_ref.shape[1]

    def copy(n):
        return pltpu.make_async_copy(
            pages_ref.at[index_ref[n]],
            states.at[n // STATE_PAGES, n % STATE_PAGES],
            sems.at[n],
        )

    @pl.when(r == 0)
    def _():
        for n in range(req * STATE_PAGES):
            copy(n).start()

    for k in range(STATE_PAGES):
        copy(r * STATE_PAGES + k).wait()

    block = GROUP_HEADS * HEAD_P
    rows = lax.broadcasted_iota(jnp.int32, (block, block), 0)
    columns = lax.broadcasted_iota(jnp.int32, (block, block), 1)
    source = ((rows >> 2) & 15) * 16 + (rows >> 6) * 4 + (rows & 3)
    perm = (columns == source).astype(jnp.float32).astype(jnp.bfloat16)
    lane = lax.broadcasted_iota(jnp.int32, (new_count, 128), 1)
    queries = q_ref[0]
    square = jnp.zeros((new_count, 128), jnp.float32)
    for g in range(groups):
        rows16 = states[r, :, 16 * g : 16 * g + 16, :].reshape(block, STATE)
        ordered = jnp.dot(perm, rows16, preferred_element_type=jnp.float32).astype(jnp.bfloat16)
        carried = lax.dot_general(queries, ordered, NT, preferred_element_type=jnp.float32)
        fade = jnp.exp(-dsc_ref[0, g])
        for pair in range(GROUP_HEADS // 2):
            cols = slice(g * block + pair * 128, g * block + pair * 128 + 128)
            factor = jnp.where(
                lane < HEAD_P, fade[:, 2 * pair : 2 * pair + 1], fade[:, 2 * pair + 1 : 2 * pair + 2]
            )
            mixed = carried[:, pair * 128 : pair * 128 + 128] * factor + fresh_ref[0, :, cols]
            gate = gate_ref[0, :, cols].astype(jnp.float32)
            gated = mixed * (gate / (1.0 + jnp.exp(-gate)))
            gated_ref[:, cols] = gated
            square = square + gated * gated
    width = gated_ref.shape[1]
    mean_square = jnp.sum(square, axis=1, keepdims=True) * (1.0 / width)
    times = lax.broadcasted_iota(jnp.int32, (new_count, 1), 0)
    scale = lax.rsqrt(mean_square + 1e-05)
    keep = times < len_ref[r]
    for c in range(width // 256):
        cols = slice(c * 256, c * 256 + 256)
        normed = gated_ref[:, cols] * scale * gain_ref[0, :, cols]
        out_ref[0, :, cols] = jnp.where(keep, normed, 0.0).astype(jnp.bfloat16)


def mixer_part(index, lengths, fresh, gate, queries, ds_cols, gain, pages):
    req, new_count, width = fresh.shape
    groups = ds_cols.shape[1]
    return pl.pallas_call(
        mixer_kernel,
        grid_spec=pltpu.PrefetchScalarGridSpec(
            num_scalar_prefetch=2,
            grid=(req,),
            in_specs=[
                pl.BlockSpec((1, new_count, width), lambda r, *_: (r, 0, 0)),
                pl.BlockSpec((1, new_count, width), lambda r, *_: (r, 0, 0)),
                pl.BlockSpec((1, new_count, STATE), lambda r, *_: (r, 0, 0)),
                pl.BlockSpec((1, groups, new_count, GROUP_HEADS), lambda r, *_: (r, 0, 0, 0)),
                pl.BlockSpec((1, 1, width), lambda r, *_: (0, 0, 0)),
                pl.BlockSpec(memory_space=pl.ANY),
            ],
            out_specs=pl.BlockSpec((1, new_count, width), lambda r, *_: (r, 0, 0)),
            scratch_shapes=[
                pltpu.VMEM((req, STATE_PAGES, PAGE, STATE), jnp.bfloat16),
                pltpu.VMEM((new_count, width), jnp.float32),
                pltpu.SemaphoreType.DMA((req * STATE_PAGES,)),
            ],
        ),
        out_shape=jax.ShapeDtypeStruct(fresh.shape, jnp.bfloat16),
        compiler_params=pltpu.CompilerParams(
            dimension_semantics=("arbitrary",), vmem_limit_bytes=VMEM_BYTES
        ),
        cost_estimate=pl.CostEstimate(
            flops=4 * req * 256 * 256 * 2048, bytes_accessed=14 << 20, transcendentals=1 << 20
        ),
        name="ssm_mix",
    )(index, lengths, fresh, gate, queries, ds_cols, gain, pages)


def softmax_step(q, kv, bias, head, acc_ref, top_ref, first):
    scores = lax.dot_general(
        q, kv[:, :HEAD_DIM], NT, preferred_element_type=jnp.float32
    )
    scores = scores * SCORE_SCALE + bias
    width = scores.shape[1] // 128
    best = jnp.max(scores, axis=1, keepdims=True)
    ones = jnp.ones((kv.shape[0], HEAD_DIM), jnp.bfloat16)
    values = jnp.concatenate([kv[:, HEAD_DIM:], ones], axis=1)
    if first:
        top = jnp.broadcast_to(best, (scores.shape[0], 128))
    else:
        old = top_ref[head]
        top = jnp.maximum(old, best)
    raised = jnp.exp2(scores - jnp.concatenate([top] * width, axis=1)).astype(jnp.bfloat16)
    summed = jnp.dot(raised, values, preferred_element_type=jnp.float32)
    if not first:
        shrink = jnp.exp2(old - top)
        summed = summed + acc_ref[head] * jnp.concatenate([shrink, shrink], axis=1)
    acc_ref[head] = summed
    top_ref[head] = top


def new_kernel(q_ref, kv_ref, acc_out, top_out):
    heads = q_ref.shape[2] // HEAD_DIM
    count = q_ref.shape[1]
    shape = (count, count)
    causal = lax.broadcasted_iota(jnp.int32, shape, 0) >= lax.broadcasted_iota(jnp.int32, shape, 1)
    bias = jnp.where(causal, 0.0, NEG)
    kv = kv_ref[0]
    for head in range(heads):
        q = q_ref[0, :, head * HEAD_DIM : (head + 1) * HEAD_DIM]
        softmax_step(q, kv, bias, head, acc_out.at[0], top_out.at[0], True)


def attend_new(queries, new_kv):
    req, count, width = queries.shape
    heads = width // HEAD_DIM
    return pl.pallas_call(
        new_kernel,
        grid=(req,),
        out_shape=(
            jax.ShapeDtypeStruct((req, heads, count, 2 * HEAD_DIM), jnp.float32),
            jax.ShapeDtypeStruct((req, heads, count, HEAD_DIM), jnp.float32),
        ),
        in_specs=[
            pl.BlockSpec((1, count, width), lambda r: (r, 0, 0)),
            pl.BlockSpec((1, count, 2 * HEAD_DIM), lambda r: (r, 0, 0)),
        ],
        out_specs=(
            pl.BlockSpec((1, heads, count, 2 * HEAD_DIM), lambda r: (r, 0, 0, 0)),
            pl.BlockSpec((1, heads, count, HEAD_DIM), lambda r: (r, 0, 0, 0)),
        ),
        compiler_params=pltpu.CompilerParams(
            dimension_semantics=("arbitrary",), vmem_limit_bytes=VMEM_BYTES
        ),
        cost_estimate=pl.CostEstimate(
            flops=8 * req * 2048 * 256 * 128, bytes_accessed=8 << 20, transcendentals=1 << 20
        ),
        name="attend_new",
    )(queries, new_kv)


def paged_kernel(last, index_ref, seen_ref, blocks_ref, len_ref, q_ref, acc_in, top_in, pages_ref, *rest):
    if last:
        out_ref, kv_buf, acc_ref, top_ref, sems = rest
    else:
        acc_out, top_out, kv_buf, sems = rest
        acc_ref, top_ref = acc_out.at[0], top_out.at[0]
    r = pl.program_id(0)
    heads = q_ref.shape[2] // HEAD_DIM
    count = q_ref.shape[1]
    per_request = index_ref.shape[0] // len_ref.shape[0]
    base = r * per_request
    blocks = blocks_ref[r]

    def copy(block, slot, i):
        return pltpu.make_async_copy(
            pages_ref.at[index_ref[base + block * BLOCK_PAGES + i]],
            kv_buf.at[slot, pl.ds(i * PAGE, PAGE)],
            sems.at[slot, i],
        )

    @pl.when(blocks > 0)
    def _():
        for i in range(BLOCK_PAGES):
            copy(0, 0, i).start()

    acc_ref[...] = acc_in[0]
    top_ref[...] = top_in[0]
    lane = lax.broadcasted_iota(jnp.int32, (1, PAGE), 1)

    def step(block, carry):
        slot = lax.rem(block, 2)

        @pl.when(block + 1 < blocks)
        def _():
            for i in range(BLOCK_PAGES):
                copy(block + 1, 1 - slot, i).start()

        for i in range(BLOCK_PAGES):
            copy(block, slot, i).wait()
        bias = jnp.concatenate(
            [
                jnp.where(lane < seen_ref[base + block * BLOCK_PAGES + i], 0.0, NEG)
                for i in range(BLOCK_PAGES)
            ],
            axis=1,
        )
        kv = kv_buf[slot]
        for head in range(heads):
            q = q_ref[0, :, head * HEAD_DIM : (head + 1) * HEAD_DIM]
            softmax_step(q, kv, bias, head, acc_ref, top_ref, False)
        return carry

    lax.fori_loop(0, blocks, step, 0)
    if last:
        keep = lax.broadcasted_iota(jnp.int32, (count, 1), 0) < len_ref[r]
        for head in range(heads):
            acc = acc_ref[head]
            result = acc[:, :HEAD_DIM] / acc[:, HEAD_DIM:]
            out_ref[0, :, head * HEAD_DIM : (head + 1) * HEAD_DIM] = jnp.where(
                keep, result, 0.0
            ).astype(jnp.bfloat16)


def attend_paged(last, index, seen, blocks, lengths, queries, acc, top, pages):
    req, count, width = queries.shape
    heads = width // HEAD_DIM
    acc_spec = pl.BlockSpec((1, heads, count, 2 * HEAD_DIM), lambda r, *_: (r, 0, 0, 0))
    top_spec = pl.BlockSpec((1, heads, count, HEAD_DIM), lambda r, *_: (r, 0, 0, 0))
    q_spec = pl.BlockSpec((1, count, width), lambda r, *_: (r, 0, 0))
    scratch = [pltpu.VMEM((2, BLOCK_PAGES * PAGE, 2 * HEAD_DIM), jnp.bfloat16)]
    if last:
        out_shape = jax.ShapeDtypeStruct(queries.shape, jnp.bfloat16)
        out_specs = q_spec
        scratch += [
            pltpu.VMEM((heads, count, 2 * HEAD_DIM), jnp.float32),
            pltpu.VMEM((heads, count, HEAD_DIM), jnp.float32),
        ]
    else:
        out_shape = (
            jax.ShapeDtypeStruct(acc.shape, jnp.float32),
            jax.ShapeDtypeStruct(top.shape, jnp.float32),
        )
        out_specs = (acc_spec, top_spec)
    return pl.pallas_call(
        functools.partial(paged_kernel, last),
        grid_spec=pltpu.PrefetchScalarGridSpec(
            num_scalar_prefetch=4,
            grid=(req,),
            in_specs=[q_spec, acc_spec, top_spec, pl.BlockSpec(memory_space=pl.ANY)],
            out_specs=out_specs,
            scratch_shapes=scratch + [pltpu.SemaphoreType.DMA((2, BLOCK_PAGES))],
        ),
        out_shape=out_shape,
        compiler_params=pltpu.CompilerParams(
            dimension_semantics=("arbitrary",), vmem_limit_bytes=VMEM_BYTES
        ),
        cost_estimate=pl.CostEstimate(
            flops=8 * req * 2048 * 1024 * 128, bytes_accessed=16 << 20, transcendentals=4 << 20
        ),
        name="attend_paged",
    )(index, seen, blocks, lengths, queries, acc, top, pages)


def page_lists(chosen, rows, seen):
    req, count = chosen.shape
    flags = chosen.astype(jnp.int32)
    place = jnp.cumsum(flags, axis=1) - flags
    hit = chosen[:, :, None] & (place[:, :, None] == jnp.arange(count, dtype=jnp.int32)[None, None, :])
    listed = jnp.sum(jnp.where(hit, rows[:, :, None], 0), axis=1)
    limits = jnp.sum(jnp.where(hit, seen[:, :, None], 0), axis=1)
    total = jnp.sum(flags, axis=1)
    valid = jnp.arange(count, dtype=jnp.int32)[None, :] < total[:, None]
    listed = jnp.where(valid, listed, listed[:, :1])
    blocks = (total + BLOCK_PAGES - 1) // BLOCK_PAGES
    return listed.reshape(-1), limits.reshape(-1), blocks


def body(
    ssm_values,
    ssm_gate,
    ssm_keys,
    ssm_queries,
    step_sizes,
    decay_rates,
    skip_weights,
    norm_gain,
    att_queries,
    new_keyvals,
    page_pool,
    page_owner,
    page_slot,
    new_lengths,
    cached_lengths,
):
    owner_count = lax.axis_size("batch")
    my_index = lax.axis_index("batch")
    req_count, new_count, width = ssm_values.shape
    head_count = decay_rates.shape[0]
    groups = head_count // GROUP_HEADS
    pool_dev = page_pool.shape[0]
    table_width = page_owner.shape[1]
    prefix_pages = table_width - STATE_PAGES
    block_rows = req_count * table_width

    owners = page_owner.reshape(block_rows)
    codes = owners * pool_dev + page_slot.reshape(block_rows)
    all_codes = lax.all_to_all(
        jnp.broadcast_to(codes[None], (owner_count, block_rows)), "batch", 0, 0, tiled=True
    )

    capacity = jnp.arange(CAP, dtype=jnp.int32)
    owned = (all_codes // pool_dev == my_index).astype(jnp.int32)
    ahead = jnp.cumsum(owned, axis=1) - owned
    picked = (owned[:, :, None] == 1) & (ahead[:, :, None] == capacity[None, None, :])
    slots = jnp.sum(jnp.where(picked, (all_codes % pool_dev)[:, :, None] + 1, 0), axis=1) - 1
    leaving = page_pool[jnp.maximum(slots.reshape(-1), 0)]
    arrived = lax.all_to_all(
        leaving.reshape((owner_count, CAP) + page_pool.shape[1:]), "batch", 0, 0, tiled=True
    )

    decay_sum = jnp.cumsum(step_sizes * decay_rates[None, None, :], axis=1)
    ds_cols = decay_sum.reshape(req_count, new_count, groups, GROUP_HEADS).transpose(0, 2, 1, 3)
    ds_rows = ds_cols.transpose(0, 1, 3, 2)
    dt_rows = step_sizes.reshape(req_count, new_count, groups, GROUP_HEADS).transpose(0, 2, 3, 1)
    skip_cols = jnp.repeat(skip_weights, HEAD_P).reshape(1, 1, width)
    fresh = fresh_part(ssm_values, ssm_keys, ssm_queries, ds_cols, ds_rows, dt_rows, skip_cols)
    acc, top = attend_new(att_queries, new_keyvals)

    order = jnp.arange(block_rows, dtype=jnp.int32)
    earlier = (owners[:, None] == owners[None, :]) & (order[None, :] < order[:, None])
    rank = jnp.sum(earlier.astype(jnp.int32), axis=1)
    landed = (owners * CAP + rank).reshape(req_count, table_width)
    seen = jnp.clip(
        cached_lengths[:, None] - jnp.arange(prefix_pages, dtype=jnp.int32)[None, :] * PAGE, 0, PAGE
    )
    listed, limits, blocks = page_lists(seen > 0, landed[:, :prefix_pages], seen)

    pages = arrived.reshape((owner_count * CAP,) + page_pool.shape[1:])
    attention = attend_paged(
        True, listed, limits, blocks, new_lengths, att_queries, acc, top, pages
    )
    mixer = mixer_part(
        landed[:, prefix_pages:].reshape(-1),
        new_lengths,
        fresh,
        ssm_gate,
        ssm_queries,
        ds_cols,
        norm_gain.reshape(1, 1, width),
        pages,
    )
    return mixer, attention


def solution(mesh):
    return jax.shard_map(
        body,
        mesh=mesh,
        in_specs=(
            P("batch", None, "head"),
            P("batch", None, "head"),
            P("batch", None, "head"),
            P("batch", None, "head"),
            P("batch", None, "head"),
            P("head"),
            P("head"),
            P("head"),
            P("batch", None, "head"),
            P("batch", None, "head"),
            P("batch", "head", None),
            P("batch", None, None),
            P("batch", None),
            P("batch"),
            P("batch"),
        ),
        out_specs=(P("batch", None, "head"), P("batch", None, "head")),
        check_vma=False,
    )
```

```python
import functools

import jax
import jax.numpy as jnp
from jax import lax
from jax.experimental import pallas as pl
from jax.experimental.pallas import tpu as pltpu
from jax.sharding import Mesh
from jax.sharding import PartitionSpec as P

HEAD_P = 64
STATE = 256
HEAD_DIM = 128
PAGE = 128
STATE_PAGES = 16
CAP = 4
DIRECT = 2
EXTRA = CAP - DIRECT
HOP_ROWS = 32
CROSS_ROWS = 24
PLANE_ROWS = 4 * EXTRA
PLANE_SIZES = (2, 3, 4, 5, PLANE_ROWS)
READY_ROWS = 4
BATCH = ("x", "z", "core")
BLOCK_PAGES = 4
GROUP_HEADS = 4
NEG = float("-inf")
SCORE_SCALE = HEAD_DIM**-0.5 * 1.4426950408889634
LOG2E = 1.4426950408889634
NT = (((1,), (1,)), ((), ()))
VMEM_BYTES = 48 * 1024 * 1024


def fresh_kernel(v_ref, k_ref, q_ref, dsc_ref, dsr_ref, dtr_ref, skip_ref, out_ref, inner_ref):
    new_count = v_ref.shape[1]

    @pl.when(pl.program_id(1) == 0)
    def _():
        inner_ref[...] = lax.dot_general(
            q_ref[0], k_ref[0], NT, preferred_element_type=jnp.float32
        )

    inner = inner_ref[...]
    shape = (new_count, new_count)
    causal = lax.broadcasted_iota(jnp.int32, shape, 0) >= lax.broadcasted_iota(jnp.int32, shape, 1)
    lane = lax.broadcasted_iota(jnp.int32, (new_count, 128), 1)
    for pair in range(GROUP_HEADS // 2):
        cols = slice(pair * 128, pair * 128 + 128)
        pair_values = v_ref[0, :, cols]
        parts = []
        for half in range(2):
            h = pair * 2 + half
            gap = dsr_ref[0, 0, h : h + 1, :] - dsc_ref[0, 0, :, h : h + 1]
            decay = jnp.exp2(jnp.where(causal, gap * LOG2E, NEG))
            weights = (decay * inner * dtr_ref[0, 0, h : h + 1, :]).astype(jnp.bfloat16)
            parts.append(jnp.dot(weights, pair_values, preferred_element_type=jnp.float32))
        fresh = jnp.where(lane < HEAD_P, parts[0], parts[1])
        out_ref[0, :, cols] = fresh + skip_ref[0, :, cols] * pair_values.astype(jnp.float32)


def fresh_part(values, keys, queries, ds_cols, ds_rows, dt_rows, skip_cols):
    req, new_count, width = values.shape
    block = GROUP_HEADS * HEAD_P
    groups = width // block
    return pl.pallas_call(
        fresh_kernel,
        grid=(req, groups),
        out_shape=jax.ShapeDtypeStruct(values.shape, jnp.float32),
        in_specs=[
            pl.BlockSpec((1, new_count, block), lambda r, g: (r, 0, g)),
            pl.BlockSpec((1, new_count, STATE), lambda r, g: (r, 0, 0)),
            pl.BlockSpec((1, new_count, STATE), lambda r, g: (r, 0, 0)),
            pl.BlockSpec((1, 1, new_count, GROUP_HEADS), lambda r, g: (r, g, 0, 0)),
            pl.BlockSpec((1, 1, GROUP_HEADS, new_count), lambda r, g: (r, g, 0, 0)),
            pl.BlockSpec((1, 1, GROUP_HEADS, new_count), lambda r, g: (r, g, 0, 0)),
            pl.BlockSpec((1, 1, block), lambda r, g: (0, 0, g)),
        ],
        out_specs=pl.BlockSpec((1, new_count, block), lambda r, g: (r, 0, g)),
        scratch_shapes=[pltpu.VMEM((new_count, new_count), jnp.float32)],
        compiler_params=pltpu.CompilerParams(
            dimension_semantics=("arbitrary", "arbitrary"), vmem_limit_bytes=VMEM_BYTES
        ),
        cost_estimate=pl.CostEstimate(
            flops=2 * req * 32 * 256 * 256 * 256, bytes_accessed=8 << 20, transcendentals=4 << 20
        ),
        name="ssm_fresh",
    )(values, keys, queries, ds_cols, ds_rows, dt_rows, skip_cols)


def mixer_kernel(
    index_ref, len_ref, fresh_ref, gate_ref, q_ref, dsc_ref, gain_ref, pages_ref, more_ref, out_ref, states, gated_ref, sems
):
    r = pl.program_id(0)
    req = states.shape[0]
    new_count = q_ref.shape[1]
    groups = dsc_ref.shape[1]

    direct = pages_ref.shape[0]

    def copy(n, source, row):
        return pltpu.make_async_copy(
            source.at[row], states.at[n // STATE_PAGES, n % STATE_PAGES], sems.at[n]
        )

    @pl.when(r == 0)
    def _():
        for n in range(req * STATE_PAGES):
            row = index_ref[n]

            @pl.when(row < direct)
            def _():
                copy(n, pages_ref, row).start()

            @pl.when(row >= direct)
            def _():
                copy(n, more_ref, row - direct).start()

    for k in range(STATE_PAGES):
        copy(r * STATE_PAGES + k, pages_ref, 0).wait()

    block = GROUP_HEADS * HEAD_P
    rows = lax.broadcasted_iota(jnp.int32, (block, block), 0)
    columns = lax.broadcasted_iota(jnp.int32, (block, block), 1)
    source = ((rows >> 2) & 15) * 16 + (rows >> 6) * 4 + (rows & 3)
    perm = (columns == source).astype(jnp.float32).astype(jnp.bfloat16)
    lane = lax.broadcasted_iota(jnp.int32, (new_count, 128), 1)
    queries = q_ref[0]
    square = jnp.zeros((new_count, 128), jnp.float32)
    for g in range(groups):
        rows16 = states[r, :, 16 * g : 16 * g + 16, :].reshape(block, STATE)
        ordered = jnp.dot(perm, rows16, preferred_element_type=jnp.float32).astype(jnp.bfloat16)
        carried = lax.dot_general(queries, ordered, NT, preferred_element_type=jnp.float32)
        fade = jnp.exp(-dsc_ref[0, g])
        for pair in range(GROUP_HEADS // 2):
            cols = slice(g * block + pair * 128, g * block + pair * 128 + 128)
            factor = jnp.where(
                lane < HEAD_P, fade[:, 2 * pair : 2 * pair + 1], fade[:, 2 * pair + 1 : 2 * pair + 2]
            )
            mixed = carried[:, pair * 128 : pair * 128 + 128] * factor + fresh_ref[0, :, cols]
            gate = gate_ref[0, :, cols].astype(jnp.float32)
            gated = mixed * (gate / (1.0 + jnp.exp(-gate)))
            gated_ref[:, cols] = gated
            square = square + gated * gated
    width = gated_ref.shape[1]
    mean_square = jnp.sum(square, axis=1, keepdims=True) * (1.0 / width)
    times = lax.broadcasted_iota(jnp.int32, (new_count, 1), 0)
    scale = lax.rsqrt(mean_square + 1e-05)
    keep = times < len_ref[r]
    for c in range(width // 256):
        cols = slice(c * 256, c * 256 + 256)
        normed = gated_ref[:, cols] * scale * gain_ref[0, :, cols]
        out_ref[0, :, cols] = jnp.where(keep, normed, 0.0).astype(jnp.bfloat16)


def mixer_part(index, lengths, fresh, gate, queries, ds_cols, gain, pages, more):
    req, new_count, width = fresh.shape
    groups = ds_cols.shape[1]
    return pl.pallas_call(
        mixer_kernel,
        grid_spec=pltpu.PrefetchScalarGridSpec(
            num_scalar_prefetch=2,
            grid=(req,),
            in_specs=[
                pl.BlockSpec((1, new_count, width), lambda r, *_: (r, 0, 0)),
                pl.BlockSpec((1, new_count, width), lambda r, *_: (r, 0, 0)),
                pl.BlockSpec((1, new_count, STATE), lambda r, *_: (r, 0, 0)),
                pl.BlockSpec((1, groups, new_count, GROUP_HEADS), lambda r, *_: (r, 0, 0, 0)),
                pl.BlockSpec((1, 1, width), lambda r, *_: (0, 0, 0)),
                pl.BlockSpec(memory_space=pl.ANY),
                pl.BlockSpec(memory_space=pl.ANY),
            ],
            out_specs=pl.BlockSpec((1, new_count, width), lambda r, *_: (r, 0, 0)),
            scratch_shapes=[
                pltpu.VMEM((req, STATE_PAGES, PAGE, STATE), jnp.bfloat16),
                pltpu.VMEM((new_count, width), jnp.float32),
                pltpu.SemaphoreType.DMA((req * STATE_PAGES,)),
            ],
        ),
        out_shape=jax.ShapeDtypeStruct(fresh.shape, jnp.bfloat16),
        compiler_params=pltpu.CompilerParams(
            dimension_semantics=("arbitrary",), vmem_limit_bytes=VMEM_BYTES
        ),
        cost_estimate=pl.CostEstimate(
            flops=4 * req * 256 * 256 * 2048, bytes_accessed=14 << 20, transcendentals=1 << 20
        ),
        name="ssm_mix",
    )(index, lengths, fresh, gate, queries, ds_cols, gain, pages, more)


def softmax_step(q, kv, bias, head, acc_ref, top_ref, first):
    scores = lax.dot_general(
        q, kv[:, :HEAD_DIM], NT, preferred_element_type=jnp.float32
    )
    scores = scores * SCORE_SCALE + bias
    width = scores.shape[1] // 128
    best = jnp.max(scores, axis=1, keepdims=True)
    ones = jnp.ones((kv.shape[0], HEAD_DIM), jnp.bfloat16)
    values = jnp.concatenate([kv[:, HEAD_DIM:], ones], axis=1)
    if first:
        top = jnp.broadcast_to(best, (scores.shape[0], 128))
    else:
        old = top_ref[head]
        top = jnp.maximum(old, best)
    raised = jnp.exp2(scores - jnp.concatenate([top] * width, axis=1)).astype(jnp.bfloat16)
    summed = jnp.dot(raised, values, preferred_element_type=jnp.float32)
    if not first:
        shrink = jnp.exp2(old - top)
        summed = summed + acc_ref[head] * jnp.concatenate([shrink, shrink], axis=1)
    acc_ref[head] = summed
    top_ref[head] = top


def new_kernel(q_ref, kv_ref, acc_out, top_out):
    heads = q_ref.shape[2] // HEAD_DIM
    count = q_ref.shape[1]
    shape = (count, count)
    causal = lax.broadcasted_iota(jnp.int32, shape, 0) >= lax.broadcasted_iota(jnp.int32, shape, 1)
    bias = jnp.where(causal, 0.0, NEG)
    kv = kv_ref[0]
    for head in range(heads):
        q = q_ref[0, :, head * HEAD_DIM : (head + 1) * HEAD_DIM]
        softmax_step(q, kv, bias, head, acc_out.at[0], top_out.at[0], True)


def attend_new(queries, new_kv):
    req, count, width = queries.shape
    heads = width // HEAD_DIM
    return pl.pallas_call(
        new_kernel,
        grid=(req,),
        out_shape=(
            jax.ShapeDtypeStruct((req, heads, count, 2 * HEAD_DIM), jnp.float32),
            jax.ShapeDtypeStruct((req, heads, count, HEAD_DIM), jnp.float32),
        ),
        in_specs=[
            pl.BlockSpec((1, count, width), lambda r: (r, 0, 0)),
            pl.BlockSpec((1, count, 2 * HEAD_DIM), lambda r: (r, 0, 0)),
        ],
        out_specs=(
            pl.BlockSpec((1, heads, count, 2 * HEAD_DIM), lambda r: (r, 0, 0, 0)),
            pl.BlockSpec((1, heads, count, HEAD_DIM), lambda r: (r, 0, 0, 0)),
        ),
        compiler_params=pltpu.CompilerParams(
            dimension_semantics=("arbitrary",), vmem_limit_bytes=VMEM_BYTES
        ),
        cost_estimate=pl.CostEstimate(
            flops=8 * req * 2048 * 256 * 128, bytes_accessed=8 << 20, transcendentals=1 << 20
        ),
        name="attend_new",
    )(queries, new_kv)


def paged_kernel(last, index_ref, seen_ref, blocks_ref, len_ref, q_ref, acc_in, top_in, pages_ref, *rest):
    if last:
        out_ref, kv_buf, acc_ref, top_ref, sems = rest
    else:
        acc_out, top_out, kv_buf, sems = rest
        acc_ref, top_ref = acc_out.at[0], top_out.at[0]
    r = pl.program_id(0)
    heads = q_ref.shape[2] // HEAD_DIM
    count = q_ref.shape[1]
    per_request = index_ref.shape[0] // len_ref.shape[0]
    base = r * per_request
    blocks = blocks_ref[r]

    def copy(block, slot, i):
        return pltpu.make_async_copy(
            pages_ref.at[index_ref[base + block * BLOCK_PAGES + i]],
            kv_buf.at[slot, pl.ds(i * PAGE, PAGE)],
            sems.at[slot, i],
        )

    @pl.when(blocks > 0)
    def _():
        for i in range(BLOCK_PAGES):
            copy(0, 0, i).start()

    acc_ref[...] = acc_in[0]
    top_ref[...] = top_in[0]
    lane = lax.broadcasted_iota(jnp.int32, (1, PAGE), 1)

    def step(block, carry):
        slot = lax.rem(block, 2)

        @pl.when(block + 1 < blocks)
        def _():
            for i in range(BLOCK_PAGES):
                copy(block + 1, 1 - slot, i).start()

        for i in range(BLOCK_PAGES):
            copy(block, slot, i).wait()
        bias = jnp.concatenate(
            [
                jnp.where(lane < seen_ref[base + block * BLOCK_PAGES + i], 0.0, NEG)
                for i in range(BLOCK_PAGES)
            ],
            axis=1,
        )
        kv = kv_buf[slot]
        for head in range(heads):
            q = q_ref[0, :, head * HEAD_DIM : (head + 1) * HEAD_DIM]
            softmax_step(q, kv, bias, head, acc_ref, top_ref, False)
        return carry

    lax.fori_loop(0, blocks, step, 0)
    if last:
        keep = lax.broadcasted_iota(jnp.int32, (count, 1), 0) < len_ref[r]
        for head in range(heads):
            acc = acc_ref[head]
            result = acc[:, :HEAD_DIM] / acc[:, HEAD_DIM:]
            out_ref[0, :, head * HEAD_DIM : (head + 1) * HEAD_DIM] = jnp.where(
                keep, result, 0.0
            ).astype(jnp.bfloat16)


def attend_paged(last, index, seen, blocks, lengths, queries, acc, top, pages):
    req, count, width = queries.shape
    heads = width // HEAD_DIM
    acc_spec = pl.BlockSpec((1, heads, count, 2 * HEAD_DIM), lambda r, *_: (r, 0, 0, 0))
    top_spec = pl.BlockSpec((1, heads, count, HEAD_DIM), lambda r, *_: (r, 0, 0, 0))
    q_spec = pl.BlockSpec((1, count, width), lambda r, *_: (r, 0, 0))
    scratch = [pltpu.VMEM((2, BLOCK_PAGES * PAGE, 2 * HEAD_DIM), jnp.bfloat16)]
    if last:
        out_shape = jax.ShapeDtypeStruct(queries.shape, jnp.bfloat16)
        out_specs = q_spec
        scratch += [
            pltpu.VMEM((heads, count, 2 * HEAD_DIM), jnp.float32),
            pltpu.VMEM((heads, count, HEAD_DIM), jnp.float32),
        ]
    else:
        out_shape = (
            jax.ShapeDtypeStruct(acc.shape, jnp.float32),
            jax.ShapeDtypeStruct(top.shape, jnp.float32),
        )
        out_specs = (acc_spec, top_spec)
    return pl.pallas_call(
        functools.partial(paged_kernel, last),
        grid_spec=pltpu.PrefetchScalarGridSpec(
            num_scalar_prefetch=4,
            grid=(req,),
            in_specs=[q_spec, acc_spec, top_spec, pl.BlockSpec(memory_space=pl.ANY)],
            out_specs=out_specs,
            scratch_shapes=scratch + [pltpu.SemaphoreType.DMA((2, BLOCK_PAGES))],
        ),
        out_shape=out_shape,
        compiler_params=pltpu.CompilerParams(
            dimension_semantics=("arbitrary",), vmem_limit_bytes=VMEM_BYTES
        ),
        cost_estimate=pl.CostEstimate(
            flops=8 * req * 2048 * 1024 * 128, bytes_accessed=16 << 20, transcendentals=4 << 20
        ),
        name="attend_paged",
    )(index, seen, blocks, lengths, queries, acc, top, pages)


def page_lists(chosen, rows, seen):
    req, count = chosen.shape
    flags = chosen.astype(jnp.int32)
    place = jnp.cumsum(flags, axis=1) - flags
    hit = chosen[:, :, None] & (place[:, :, None] == jnp.arange(count, dtype=jnp.int32)[None, None, :])
    listed = jnp.sum(jnp.where(hit, rows[:, :, None], 0), axis=1)
    limits = jnp.sum(jnp.where(hit, seen[:, :, None], 0), axis=1)
    total = jnp.sum(flags, axis=1)
    valid = jnp.arange(count, dtype=jnp.int32)[None, :] < total[:, None]
    listed = jnp.where(valid, listed, listed[:, :1])
    blocks = (total + BLOCK_PAGES - 1) // BLOCK_PAGES
    return listed.reshape(-1), limits.reshape(-1), blocks


def flip(array, axis, own):
    return jnp.where(own == 1, jnp.flip(array, axis), array)


def exclusive(counts, axis=0):
    return jnp.cumsum(counts, axis=axis) - counts


def place_rows(starts, counts, values, length):
    extra = jnp.arange(EXTRA, dtype=jnp.int32)
    where = starts[..., None] + extra
    where = jnp.where(extra < counts[..., None], where, -1)
    flat = starts.shape[:-1] + (starts.shape[-1] * EXTRA, 1)
    hit = where.reshape(flat) == jnp.arange(length, dtype=jnp.int32)
    return jnp.sum(jnp.where(hit, values.reshape(flat), 0), axis=-2)


def exchange_tables(codes, planes, my_x, my_core):
    return lax.all_to_all(
        jnp.broadcast_to(codes[None], (planes * 4, codes.shape[0])), BATCH, 0, 0, tiled=True
    )


def body(
    ssm_values,
    ssm_gate,
    ssm_keys,
    ssm_queries,
    step_sizes,
    decay_rates,
    skip_weights,
    norm_gain,
    att_queries,
    new_keyvals,
    page_pool,
    page_owner,
    page_slot,
    new_lengths,
    cached_lengths,
):
    planes = lax.axis_size("z")
    my_x, my_z, my_core = lax.axis_index("x"), lax.axis_index("z"), lax.axis_index("core")
    owner_count = planes * 4
    my_index = (my_x * planes + my_z) * 2 + my_core
    req_count, new_count, width = ssm_values.shape
    head_count = decay_rates.shape[0]
    groups = head_count // GROUP_HEADS
    pool_dev = page_pool.shape[0]
    page_shape = page_pool.shape[1:]
    table_width = page_owner.shape[1]
    prefix_pages = table_width - STATE_PAGES
    block_rows = req_count * table_width

    seen = jnp.clip(
        cached_lengths[:, None] - jnp.arange(prefix_pages, dtype=jnp.int32)[None, :] * PAGE, 0, PAGE
    )
    table = page_owner.reshape(req_count, table_width) * pool_dev + page_slot
    codes = jnp.concatenate(
        [
            jnp.where(seen > 0, table[:, :prefix_pages], -1).reshape(-1),
            table[:, prefix_pages:].reshape(-1),
        ]
    )
    all_codes = exchange_tables(codes, planes, my_x, my_core)
    all_owners = jnp.where(all_codes < 0, -1, all_codes // pool_dev)

    capacity = jnp.arange(CAP, dtype=jnp.int32)
    owned = (all_owners == my_index).astype(jnp.int32)
    ahead = exclusive(owned, 1)
    picked = (owned[:, :, None] == 1) & (ahead[:, :, None] == capacity[None, None, :])
    slots = jnp.sum(jnp.where(picked, (all_codes % pool_dev)[:, :, None], 0), axis=1)
    leaving = page_pool[slots[:, :DIRECT].reshape(-1)]
    arrived = lax.all_to_all(
        leaving.reshape((owner_count, DIRECT) + page_shape), BATCH, 0, 0, tiled=True
    ).reshape((owner_count * DIRECT,) + page_shape)

    named = all_owners[None, :, :] == jnp.arange(owner_count, dtype=jnp.int32)[:, None, None]
    demand = jnp.sum(named.astype(jnp.int32), axis=2)
    extra = jnp.clip(demand - DIRECT, 0, EXTRA).reshape(2, planes, 2, 2, planes, 2)
    most = jnp.max(jnp.sum(extra, axis=(0, 2)))
    near = lax.dynamic_index_in_dim(extra, my_z, 1, keepdims=False)
    near = flip(flip(flip(flip(near, 0, my_x), 2, my_x), 1, my_core), 4, my_core)
    rest = slots.reshape(2, planes, 2, CAP)[..., DIRECT:]
    rest = flip(flip(rest, 0, my_x), 2, my_core)
    steps = jnp.arange(EXTRA, dtype=jnp.int32)

    core_send = near[0, 0, :, :, 1].reshape(-1)
    core_rows = place_rows(exclusive(core_send), core_send, rest[:, :, 1].reshape(-1, EXTRA), HOP_ROWS)
    from_core = lax.ppermute(page_pool[core_rows], "core", [(0, 1), (1, 0)])
    core_recv = near[0, 1, :, :, 0].reshape(-1)
    core_at = exclusive(core_recv).reshape(2, planes)[:, :, None] + steps + pool_dev
    held = jnp.concatenate([page_pool, from_core])

    cross_send = near[0, :, 1, :, 0].T.reshape(-1)
    cross_values = jnp.stack([rest[1, :, 0], core_at[1]], axis=1).reshape(-1, EXTRA)
    cross_rows = place_rows(exclusive(cross_send), cross_send, cross_values, HOP_ROWS)
    crossing_pages, att_queries, ssm_values = lax.optimization_barrier(
        (held[cross_rows[:CROSS_ROWS]], att_queries, ssm_values)
    )
    from_cross = lax.ppermute(crossing_pages, "x", [(0, 1), (1, 0)])
    cross_recv = near[1, :, 0, :, 0].T.reshape(-1)
    cross_at = exclusive(cross_recv).reshape(planes, 2)[:, :, None] + steps + pool_dev + HOP_ROWS
    crossing = jnp.max(
        jnp.sum(jnp.stack([extra[0, :, :, 1], extra[1, :, :, 0]]), axis=(2, 3))
    )
    local = held
    held = jnp.concatenate([local, from_cross])

    plane_send = near[:, :, 0, :, 0].reshape(4, planes).T
    plane_values = jnp.concatenate(
        [rest[0, :, 0][:, None], core_at[0][:, None], cross_at], axis=1
    )
    plane_rows = place_rows(exclusive(plane_send, 1), plane_send, plane_values, PLANE_ROWS)
    ready = held[plane_rows[:, :READY_ROWS].reshape(-1)]
    ready = lax.optimization_barrier(ready).reshape((planes, READY_ROWS) + page_shape)

    owners = codes // pool_dev
    wanted = codes >= 0
    order = jnp.arange(block_rows, dtype=jnp.int32)
    same = (owners[:, None] == owners[None, :]) & wanted[:, None] & wanted[None, :]
    rank = jnp.sum((same & (order[None, :] < order[:, None])).astype(jnp.int32), axis=1)
    mine = jnp.sum(
        jnp.where(jnp.arange(owner_count) == my_index, extra.reshape(owner_count, owner_count), 0), axis=1
    ).reshape(2, planes, 2)
    mine = flip(flip(mine, 0, my_x), 2, my_core).transpose(1, 0, 2).reshape(planes, 4)
    begin = exclusive(mine, 1).reshape(planes, 2, 2).transpose(1, 0, 2)
    begin = flip(flip(begin, 0, my_x), 2, my_core).reshape(owner_count)
    owner_hit = owners[:, None] == jnp.arange(owner_count, dtype=jnp.int32)[None, :]
    begin = jnp.sum(jnp.where(owner_hit, begin[None, :], 0), axis=1)
    is_direct = rank < DIRECT
    direct_at = owners * DIRECT + rank
    plane_of = (owners // 2) % planes
    plane_at = begin + rank - DIRECT
    prefix_count = req_count * prefix_pages
    shape = (req_count, prefix_pages)
    prefix_direct = (is_direct & wanted)[:prefix_count].reshape(shape)
    first_lists = page_lists(prefix_direct, direct_at[:prefix_count].reshape(shape), seen)

    decay_sum = jnp.cumsum(step_sizes * decay_rates[None, None, :], axis=1)
    ds_cols = decay_sum.reshape(req_count, new_count, groups, GROUP_HEADS).transpose(0, 2, 1, 3)
    ds_rows = ds_cols.transpose(0, 1, 3, 2)
    dt_rows = step_sizes.reshape(req_count, new_count, groups, GROUP_HEADS).transpose(0, 2, 3, 1)
    skip_cols = jnp.repeat(skip_weights, HEAD_P).reshape(1, 1, width)
    fresh = fresh_part(ssm_values, ssm_keys, ssm_queries, ds_cols, ds_rows, dt_rows, skip_cols)
    acc, top = attend_new(att_queries, new_keyvals)

    def finish(size):
        def run():
            if size <= READY_ROWS:
                going = ready[:, :size]
            else:
                source = held
                if size == PLANE_ROWS:
                    others = lax.ppermute(local[cross_rows[CROSS_ROWS:]], "x", [(0, 1), (1, 0)])
                    source = jnp.concatenate([held, others])
                going = source[plane_rows[:, :size].reshape(-1)]
                going = going.reshape((planes, size) + page_shape)
            come = lax.all_to_all(going, "z", 0, 0, tiled=True)
            come = come.reshape((planes * size,) + page_shape)
            acc_1, top_1 = attend_paged(
                False, *first_lists, new_lengths, att_queries, acc, top, arrived
            )
            late_at = plane_of * size + plane_at
            late = (wanted & ~is_direct)[:prefix_count].reshape(shape)
            last_lists = page_lists(late, late_at[:prefix_count].reshape(shape), seen)
            landed = jnp.where(is_direct, direct_at, owner_count * DIRECT + late_at)
            attention = attend_paged(
                True, *last_lists, new_lengths, att_queries, acc_1, top_1, come
            )
            mixer = mixer_part(
                landed[prefix_count:],
                new_lengths,
                fresh,
                ssm_gate,
                ssm_queries,
                ds_cols,
                norm_gain.reshape(1, 1, width),
                arrived,
                come,
            )
            return mixer, attention

        return run

    choice = sum([(most > size).astype(jnp.int32) for size in PLANE_SIZES[:-1]])
    choice = jnp.where(crossing > CROSS_ROWS, len(PLANE_SIZES) - 1, choice)
    return lax.switch(choice, [finish(size) for size in PLANE_SIZES])


def solution(mesh):
    devices = mesh.devices
    split = Mesh(
        devices.reshape(2, devices.shape[0] // 4, 2, devices.shape[1]), BATCH + ("head",)
    )
    return jax.shard_map(
        body,
        mesh=split,
        in_specs=(
            P(BATCH, None, "head"),
            P(BATCH, None, "head"),
            P(BATCH, None, "head"),
            P(BATCH, None, "head"),
            P(BATCH, None, "head"),
            P("head"),
            P("head"),
            P("head"),
            P(BATCH, None, "head"),
            P(BATCH, None, "head"),
            P(BATCH, "head", None),
            P(BATCH, None, None),
            P(BATCH, None),
            P(BATCH),
            P(BATCH),
        ),
        out_specs=(P(BATCH, None, "head"), P(BATCH, None, "head")),
        check_vma=False,
    )
```

```python
import functools

import jax
import jax.numpy as jnp
from jax import lax
from jax.experimental import pallas as pl
from jax.experimental.pallas import tpu as pltpu
from jax.sharding import Mesh
from jax.sharding import PartitionSpec as P

HEAD_P = 64
STATE = 256
HEAD_DIM = 128
PAGE = 128
STATE_PAGES = 16
CAP = 4
DIRECT = 2
EXTRA = CAP - DIRECT
HOP_ROWS = 32
CROSS_ROWS = 24
PLANE_ROWS = 4 * EXTRA
READY_ROWS = 3
LATE_ROWS = PLANE_ROWS - READY_ROWS
BATCH = ("x", "z", "core")
BLOCK_PAGES = 4
GROUP_HEADS = 4
NEG = float("-inf")
SCORE_SCALE = HEAD_DIM**-0.5 * 1.4426950408889634
LOG2E = 1.4426950408889634
NT = (((1,), (1,)), ((), ()))
VMEM_BYTES = 48 * 1024 * 1024


def fresh_kernel(v_ref, k_ref, q_ref, dsc_ref, dsr_ref, dtr_ref, skip_ref, out_ref, inner_ref):
    new_count = v_ref.shape[1]

    @pl.when(pl.program_id(1) == 0)
    def _():
        inner_ref[...] = lax.dot_general(
            q_ref[0], k_ref[0], NT, preferred_element_type=jnp.float32
        )

    inner = inner_ref[...]
    shape = (new_count, new_count)
    causal = lax.broadcasted_iota(jnp.int32, shape, 0) >= lax.broadcasted_iota(jnp.int32, shape, 1)
    lane = lax.broadcasted_iota(jnp.int32, (new_count, 128), 1)
    for pair in range(GROUP_HEADS // 2):
        cols = slice(pair * 128, pair * 128 + 128)
        pair_values = v_ref[0, :, cols]
        parts = []
        for half in range(2):
            h = pair * 2 + half
            gap = dsr_ref[0, 0, h : h + 1, :] - dsc_ref[0, 0, :, h : h + 1]
            decay = jnp.exp2(jnp.where(causal, gap * LOG2E, NEG))
            weights = (decay * inner * dtr_ref[0, 0, h : h + 1, :]).astype(jnp.bfloat16)
            parts.append(jnp.dot(weights, pair_values, preferred_element_type=jnp.float32))
        fresh = jnp.where(lane < HEAD_P, parts[0], parts[1])
        out_ref[0, :, cols] = fresh + skip_ref[0, :, cols] * pair_values.astype(jnp.float32)


def fresh_part(values, keys, queries, ds_cols, ds_rows, dt_rows, skip_cols):
    req, new_count, width = values.shape
    block = GROUP_HEADS * HEAD_P
    groups = width // block
    return pl.pallas_call(
        fresh_kernel,
        grid=(req, groups),
        out_shape=jax.ShapeDtypeStruct(values.shape, jnp.float32),
        in_specs=[
            pl.BlockSpec((1, new_count, block), lambda r, g: (r, 0, g)),
            pl.BlockSpec((1, new_count, STATE), lambda r, g: (r, 0, 0)),
            pl.BlockSpec((1, new_count, STATE), lambda r, g: (r, 0, 0)),
            pl.BlockSpec((1, 1, new_count, GROUP_HEADS), lambda r, g: (r, g, 0, 0)),
            pl.BlockSpec((1, 1, GROUP_HEADS, new_count), lambda r, g: (r, g, 0, 0)),
            pl.BlockSpec((1, 1, GROUP_HEADS, new_count), lambda r, g: (r, g, 0, 0)),
            pl.BlockSpec((1, 1, block), lambda r, g: (0, 0, g)),
        ],
        out_specs=pl.BlockSpec((1, new_count, block), lambda r, g: (r, 0, g)),
        scratch_shapes=[pltpu.VMEM((new_count, new_count), jnp.float32)],
        compiler_params=pltpu.CompilerParams(
            dimension_semantics=("arbitrary", "arbitrary"), vmem_limit_bytes=VMEM_BYTES
        ),
        cost_estimate=pl.CostEstimate(
            flops=2 * req * 32 * 256 * 256 * 256, bytes_accessed=8 << 20, transcendentals=4 << 20
        ),
        name="ssm_fresh",
    )(values, keys, queries, ds_cols, ds_rows, dt_rows, skip_cols)


def start_from(sources, row, make):
    base = 0
    for source in sources:
        count = source.shape[0]
        here = row - base

        @pl.when((here >= 0) & (here < count))
        def _():
            make(source.at[here]).start()

        base += count


def mixer_kernel(
    index_ref, len_ref, fresh_ref, gate_ref, q_ref, dsc_ref, gain_ref, *rest
):
    *sources, out_ref, states, gated_ref, sems = rest
    r = pl.program_id(0)
    req = states.shape[0]
    new_count = q_ref.shape[1]
    groups = dsc_ref.shape[1]

    def make(n):
        return lambda page: pltpu.make_async_copy(
            page, states.at[n // STATE_PAGES, n % STATE_PAGES], sems.at[n]
        )

    @pl.when(r == 0)
    def _():
        for n in range(req * STATE_PAGES):
            start_from(sources, index_ref[n], make(n))

    for k in range(STATE_PAGES):
        make(r * STATE_PAGES + k)(sources[0].at[0]).wait()

    block = GROUP_HEADS * HEAD_P
    rows = lax.broadcasted_iota(jnp.int32, (block, block), 0)
    columns = lax.broadcasted_iota(jnp.int32, (block, block), 1)
    source = ((rows >> 2) & 15) * 16 + (rows >> 6) * 4 + (rows & 3)
    perm = (columns == source).astype(jnp.float32).astype(jnp.bfloat16)
    lane = lax.broadcasted_iota(jnp.int32, (new_count, 128), 1)
    queries = q_ref[0]
    square = jnp.zeros((new_count, 128), jnp.float32)
    for g in range(groups):
        rows16 = states[r, :, 16 * g : 16 * g + 16, :].reshape(block, STATE)
        ordered = jnp.dot(perm, rows16, preferred_element_type=jnp.float32).astype(jnp.bfloat16)
        carried = lax.dot_general(queries, ordered, NT, preferred_element_type=jnp.float32)
        fade = jnp.exp(-dsc_ref[0, g])
        for pair in range(GROUP_HEADS // 2):
            cols = slice(g * block + pair * 128, g * block + pair * 128 + 128)
            factor = jnp.where(
                lane < HEAD_P, fade[:, 2 * pair : 2 * pair + 1], fade[:, 2 * pair + 1 : 2 * pair + 2]
            )
            mixed = carried[:, pair * 128 : pair * 128 + 128] * factor + fresh_ref[0, :, cols]
            gate = gate_ref[0, :, cols].astype(jnp.float32)
            gated = mixed * (gate / (1.0 + jnp.exp(-gate)))
            gated_ref[:, cols] = gated
            square = square + gated * gated
    width = gated_ref.shape[1]
    mean_square = jnp.sum(square, axis=1, keepdims=True) * (1.0 / width)
    times = lax.broadcasted_iota(jnp.int32, (new_count, 1), 0)
    scale = lax.rsqrt(mean_square + 1e-05)
    keep = times < len_ref[r]
    for c in range(width // 256):
        cols = slice(c * 256, c * 256 + 256)
        normed = gated_ref[:, cols] * scale * gain_ref[0, :, cols]
        out_ref[0, :, cols] = jnp.where(keep, normed, 0.0).astype(jnp.bfloat16)


def mixer_part(index, lengths, fresh, gate, queries, ds_cols, gain, sources):
    req, new_count, width = fresh.shape
    groups = ds_cols.shape[1]
    return pl.pallas_call(
        mixer_kernel,
        grid_spec=pltpu.PrefetchScalarGridSpec(
            num_scalar_prefetch=2,
            grid=(req,),
            in_specs=[
                pl.BlockSpec((1, new_count, width), lambda r, *_: (r, 0, 0)),
                pl.BlockSpec((1, new_count, width), lambda r, *_: (r, 0, 0)),
                pl.BlockSpec((1, new_count, STATE), lambda r, *_: (r, 0, 0)),
                pl.BlockSpec((1, groups, new_count, GROUP_HEADS), lambda r, *_: (r, 0, 0, 0)),
                pl.BlockSpec((1, 1, width), lambda r, *_: (0, 0, 0)),
            ]
            + [pl.BlockSpec(memory_space=pl.ANY)] * len(sources),
            out_specs=pl.BlockSpec((1, new_count, width), lambda r, *_: (r, 0, 0)),
            scratch_shapes=[
                pltpu.VMEM((req, STATE_PAGES, PAGE, STATE), jnp.bfloat16),
                pltpu.VMEM((new_count, width), jnp.float32),
                pltpu.SemaphoreType.DMA((req * STATE_PAGES,)),
            ],
        ),
        out_shape=jax.ShapeDtypeStruct(fresh.shape, jnp.bfloat16),
        compiler_params=pltpu.CompilerParams(
            dimension_semantics=("arbitrary",), vmem_limit_bytes=VMEM_BYTES
        ),
        cost_estimate=pl.CostEstimate(
            flops=4 * req * 256 * 256 * 2048, bytes_accessed=14 << 20, transcendentals=1 << 20
        ),
        name="ssm_mix",
    )(index, lengths, fresh, gate, queries, ds_cols, gain, *sources)


def softmax_step(q, kv, bias, head, acc_ref, top_ref, first):
    scores = lax.dot_general(
        q, kv[:, :HEAD_DIM], NT, preferred_element_type=jnp.float32
    )
    scores = scores * SCORE_SCALE + bias
    width = scores.shape[1] // 128
    best = jnp.max(scores, axis=1, keepdims=True)
    ones = jnp.ones((kv.shape[0], HEAD_DIM), jnp.bfloat16)
    values = jnp.concatenate([kv[:, HEAD_DIM:], ones], axis=1)
    if first:
        top = jnp.broadcast_to(best, (scores.shape[0], 128))
    else:
        old = top_ref[head]
        top = jnp.maximum(old, best)
    raised = jnp.exp2(scores - jnp.concatenate([top] * width, axis=1)).astype(jnp.bfloat16)
    summed = jnp.dot(raised, values, preferred_element_type=jnp.float32)
    if not first:
        shrink = jnp.exp2(old - top)
        summed = summed + acc_ref[head] * jnp.concatenate([shrink, shrink], axis=1)
    acc_ref[head] = summed
    top_ref[head] = top


def new_kernel(q_ref, kv_ref, acc_out, top_out):
    heads = q_ref.shape[2] // HEAD_DIM
    count = q_ref.shape[1]
    shape = (count, count)
    causal = lax.broadcasted_iota(jnp.int32, shape, 0) >= lax.broadcasted_iota(jnp.int32, shape, 1)
    bias = jnp.where(causal, 0.0, NEG)
    kv = kv_ref[0]
    for head in range(heads):
        q = q_ref[0, :, head * HEAD_DIM : (head + 1) * HEAD_DIM]
        softmax_step(q, kv, bias, head, acc_out.at[0], top_out.at[0], True)


def attend_new(queries, new_kv):
    req, count, width = queries.shape
    heads = width // HEAD_DIM
    return pl.pallas_call(
        new_kernel,
        grid=(req,),
        out_shape=(
            jax.ShapeDtypeStruct((req, heads, count, 2 * HEAD_DIM), jnp.float32),
            jax.ShapeDtypeStruct((req, heads, count, HEAD_DIM), jnp.float32),
        ),
        in_specs=[
            pl.BlockSpec((1, count, width), lambda r: (r, 0, 0)),
            pl.BlockSpec((1, count, 2 * HEAD_DIM), lambda r: (r, 0, 0)),
        ],
        out_specs=(
            pl.BlockSpec((1, heads, count, 2 * HEAD_DIM), lambda r: (r, 0, 0, 0)),
            pl.BlockSpec((1, heads, count, HEAD_DIM), lambda r: (r, 0, 0, 0)),
        ),
        compiler_params=pltpu.CompilerParams(
            dimension_semantics=("arbitrary",), vmem_limit_bytes=VMEM_BYTES
        ),
        cost_estimate=pl.CostEstimate(
            flops=8 * req * 2048 * 256 * 128, bytes_accessed=8 << 20, transcendentals=1 << 20
        ),
        name="attend_new",
    )(queries, new_kv)


def paged_kernel(last, source_count, index_ref, seen_ref, blocks_ref, len_ref, q_ref, acc_in, top_in, *rest):
    sources, rest = rest[:source_count], rest[source_count:]
    if last:
        out_ref, kv_buf, acc_ref, top_ref, sems = rest
    else:
        acc_out, top_out, kv_buf, sems = rest
        acc_ref, top_ref = acc_out.at[0], top_out.at[0]
    r = pl.program_id(0)
    heads = q_ref.shape[2] // HEAD_DIM
    count = q_ref.shape[1]
    per_request = index_ref.shape[0] // len_ref.shape[0]
    base = r * per_request
    blocks = blocks_ref[r]

    def make(slot, i):
        return lambda page: pltpu.make_async_copy(
            page, kv_buf.at[slot, pl.ds(i * PAGE, PAGE)], sems.at[slot, i]
        )

    def fetch(block, slot):
        for i in range(BLOCK_PAGES):
            start_from(sources, index_ref[base + block * BLOCK_PAGES + i], make(slot, i))

    @pl.when(blocks > 0)
    def _():
        fetch(0, 0)

    acc_ref[...] = acc_in[0]
    top_ref[...] = top_in[0]
    lane = lax.broadcasted_iota(jnp.int32, (1, PAGE), 1)

    def step(block, carry):
        slot = lax.rem(block, 2)

        @pl.when(block + 1 < blocks)
        def _():
            fetch(block + 1, 1 - slot)

        for i in range(BLOCK_PAGES):
            make(slot, i)(sources[0].at[0]).wait()
        bias = jnp.concatenate(
            [
                jnp.where(lane < seen_ref[base + block * BLOCK_PAGES + i], 0.0, NEG)
                for i in range(BLOCK_PAGES)
            ],
            axis=1,
        )
        kv = kv_buf[slot]
        for head in range(heads):
            q = q_ref[0, :, head * HEAD_DIM : (head + 1) * HEAD_DIM]
            softmax_step(q, kv, bias, head, acc_ref, top_ref, False)
        return carry

    lax.fori_loop(0, blocks, step, 0)
    if last:
        keep = lax.broadcasted_iota(jnp.int32, (count, 1), 0) < len_ref[r]
        for head in range(heads):
            acc = acc_ref[head]
            result = acc[:, :HEAD_DIM] / acc[:, HEAD_DIM:]
            out_ref[0, :, head * HEAD_DIM : (head + 1) * HEAD_DIM] = jnp.where(
                keep, result, 0.0
            ).astype(jnp.bfloat16)


def attend_paged(last, index, seen, blocks, lengths, queries, acc, top, sources):
    req, count, width = queries.shape
    heads = width // HEAD_DIM
    acc_spec = pl.BlockSpec((1, heads, count, 2 * HEAD_DIM), lambda r, *_: (r, 0, 0, 0))
    top_spec = pl.BlockSpec((1, heads, count, HEAD_DIM), lambda r, *_: (r, 0, 0, 0))
    q_spec = pl.BlockSpec((1, count, width), lambda r, *_: (r, 0, 0))
    scratch = [pltpu.VMEM((2, BLOCK_PAGES * PAGE, 2 * HEAD_DIM), jnp.bfloat16)]
    if last:
        out_shape = jax.ShapeDtypeStruct(queries.shape, jnp.bfloat16)
        out_specs = q_spec
        scratch += [
            pltpu.VMEM((heads, count, 2 * HEAD_DIM), jnp.float32),
            pltpu.VMEM((heads, count, HEAD_DIM), jnp.float32),
        ]
    else:
        out_shape = (
            jax.ShapeDtypeStruct(acc.shape, jnp.float32),
            jax.ShapeDtypeStruct(top.shape, jnp.float32),
        )
        out_specs = (acc_spec, top_spec)
    return pl.pallas_call(
        functools.partial(paged_kernel, last, len(sources)),
        grid_spec=pltpu.PrefetchScalarGridSpec(
            num_scalar_prefetch=4,
            grid=(req,),
            in_specs=[q_spec, acc_spec, top_spec]
            + [pl.BlockSpec(memory_space=pl.ANY)] * len(sources),
            out_specs=out_specs,
            scratch_shapes=scratch + [pltpu.SemaphoreType.DMA((2, BLOCK_PAGES))],
        ),
        out_shape=out_shape,
        compiler_params=pltpu.CompilerParams(
            dimension_semantics=("arbitrary",), vmem_limit_bytes=VMEM_BYTES
        ),
        cost_estimate=pl.CostEstimate(
            flops=8 * req * 2048 * 1024 * 128, bytes_accessed=16 << 20, transcendentals=4 << 20
        ),
        name="attend_paged",
    )(index, seen, blocks, lengths, queries, acc, top, *sources)


def page_lists(chosen, rows, seen):
    req, count = chosen.shape
    flags = chosen.astype(jnp.int32)
    place = jnp.cumsum(flags, axis=1) - flags
    hit = chosen[:, :, None] & (place[:, :, None] == jnp.arange(count, dtype=jnp.int32)[None, None, :])
    listed = jnp.sum(jnp.where(hit, rows[:, :, None], 0), axis=1)
    limits = jnp.sum(jnp.where(hit, seen[:, :, None], 0), axis=1)
    total = jnp.sum(flags, axis=1)
    valid = jnp.arange(count, dtype=jnp.int32)[None, :] < total[:, None]
    listed = jnp.where(valid, listed, listed[:, :1])
    blocks = (total + BLOCK_PAGES - 1) // BLOCK_PAGES
    return listed.reshape(-1), limits.reshape(-1), blocks


def flip(array, axis, own):
    return jnp.where(own == 1, jnp.flip(array, axis), array)


def exclusive(counts, axis=0):
    return jnp.cumsum(counts, axis=axis) - counts


def place_rows(starts, counts, values, length):
    extra = jnp.arange(EXTRA, dtype=jnp.int32)
    where = starts[..., None] + extra
    where = jnp.where(extra < counts[..., None], where, -1)
    flat = starts.shape[:-1] + (starts.shape[-1] * EXTRA, 1)
    hit = where.reshape(flat) == jnp.arange(length, dtype=jnp.int32)
    return jnp.sum(jnp.where(hit, values.reshape(flat), 0), axis=-2)


def exchange_tables(codes, planes, my_x, my_core):
    return lax.all_to_all(
        jnp.broadcast_to(codes[None], (planes * 4, codes.shape[0])), BATCH, 0, 0, tiled=True
    )


def pick(rows, *sources):
    picked = None
    base = 0
    for source in sources:
        count = source.shape[0]
        here = source[jnp.clip(rows - base, 0, count - 1)]
        picked = here if picked is None else jnp.where((rows < base)[:, None, None], picked, here)
        base += count
    return picked


def body(
    ssm_values,
    ssm_gate,
    ssm_keys,
    ssm_queries,
    step_sizes,
    decay_rates,
    skip_weights,
    norm_gain,
    att_queries,
    new_keyvals,
    page_pool,
    page_owner,
    page_slot,
    new_lengths,
    cached_lengths,
):
    planes = lax.axis_size("z")
    my_x, my_z, my_core = lax.axis_index("x"), lax.axis_index("z"), lax.axis_index("core")
    owner_count = planes * 4
    my_index = (my_x * planes + my_z) * 2 + my_core
    req_count, new_count, width = ssm_values.shape
    head_count = decay_rates.shape[0]
    groups = head_count // GROUP_HEADS
    pool_dev = page_pool.shape[0]
    page_shape = page_pool.shape[1:]
    table_width = page_owner.shape[1]
    prefix_pages = table_width - STATE_PAGES
    block_rows = req_count * table_width

    seen = jnp.clip(
        cached_lengths[:, None] - jnp.arange(prefix_pages, dtype=jnp.int32)[None, :] * PAGE, 0, PAGE
    )
    table = page_owner.reshape(req_count, table_width) * pool_dev + page_slot
    codes = jnp.concatenate(
        [
            jnp.where(seen > 0, table[:, :prefix_pages], -1).reshape(-1),
            table[:, prefix_pages:].reshape(-1),
        ]
    )
    all_codes = exchange_tables(codes, planes, my_x, my_core)
    all_owners = jnp.where(all_codes < 0, -1, all_codes // pool_dev)

    capacity = jnp.arange(CAP, dtype=jnp.int32)
    owned = (all_owners == my_index).astype(jnp.int32)
    ahead = exclusive(owned, 1)
    picked = (owned[:, :, None] == 1) & (ahead[:, :, None] == capacity[None, None, :])
    slots = jnp.sum(jnp.where(picked, (all_codes % pool_dev)[:, :, None], 0), axis=1)
    leaving = page_pool[slots[:, :DIRECT].reshape(-1)]
    leaving, page_pool = lax.optimization_barrier((leaving, page_pool))
    arrived = lax.all_to_all(
        leaving.reshape((owner_count, DIRECT) + page_shape), BATCH, 0, 0, tiled=True
    ).reshape((owner_count * DIRECT,) + page_shape)

    named = all_owners[None, :, :] == jnp.arange(owner_count, dtype=jnp.int32)[:, None, None]
    demand = jnp.sum(named.astype(jnp.int32), axis=2)
    extra = jnp.clip(demand - DIRECT, 0, EXTRA).reshape(2, planes, 2, 2, planes, 2)
    most = jnp.max(jnp.sum(extra, axis=(0, 2)))
    near = lax.dynamic_index_in_dim(extra, my_z, 1, keepdims=False)
    near = flip(flip(flip(flip(near, 0, my_x), 2, my_x), 1, my_core), 4, my_core)
    rest = slots.reshape(2, planes, 2, CAP)[..., DIRECT:]
    rest = flip(flip(rest, 0, my_x), 2, my_core)
    steps = jnp.arange(EXTRA, dtype=jnp.int32)

    core_send = near[0, 0, :, :, 1].reshape(-1)
    core_rows = place_rows(exclusive(core_send), core_send, rest[:, :, 1].reshape(-1, EXTRA), HOP_ROWS)
    from_core = lax.ppermute(page_pool[core_rows], "core", [(0, 1), (1, 0)])
    core_recv = near[0, 1, :, :, 0].reshape(-1)
    core_at = exclusive(core_recv).reshape(2, planes)[:, :, None] + steps + pool_dev

    cross_send = near[0, :, 1, :, 0].T.reshape(-1)
    cross_values = jnp.stack([rest[1, :, 0], core_at[1]], axis=1).reshape(-1, EXTRA)
    cross_rows = place_rows(exclusive(cross_send), cross_send, cross_values, HOP_ROWS)
    crossing_pages, att_queries, ssm_values = lax.optimization_barrier(
        (pick(cross_rows[:CROSS_ROWS], page_pool, from_core), att_queries, ssm_values)
    )
    from_cross = lax.ppermute(crossing_pages, "x", [(0, 1), (1, 0)])
    cross_recv = near[1, :, 0, :, 0].T.reshape(-1)
    cross_at = exclusive(cross_recv).reshape(planes, 2)[:, :, None] + steps + pool_dev + HOP_ROWS
    crossing = jnp.max(
        jnp.sum(jnp.stack([extra[0, :, :, 1], extra[1, :, :, 0]]), axis=(2, 3))
    )
    cross_more = lax.cond(
        crossing > CROSS_ROWS,
        lambda: lax.ppermute(
            pick(cross_rows[CROSS_ROWS:], page_pool, from_core), "x", [(0, 1), (1, 0)]
        ),
        lambda: from_core[: HOP_ROWS - CROSS_ROWS],
    )

    plane_send = near[:, :, 0, :, 0].reshape(4, planes).T
    plane_values = jnp.concatenate(
        [rest[0, :, 0][:, None], core_at[0][:, None], cross_at], axis=1
    )
    plane_rows = place_rows(exclusive(plane_send, 1), plane_send, plane_values, PLANE_ROWS)
    ready = pick(
        plane_rows[:, :READY_ROWS].reshape(-1), page_pool, from_core, from_cross, cross_more
    )
    ready, arrived, late_queries = lax.optimization_barrier((ready, arrived, att_queries))
    come = lax.all_to_all(
        ready.reshape((planes, READY_ROWS) + page_shape), "z", 0, 0, tiled=True
    ).reshape((planes * READY_ROWS,) + page_shape)
    come, late_rows = lax.optimization_barrier((come, plane_rows[:, READY_ROWS:]))

    owners = codes // pool_dev
    wanted = codes >= 0
    order = jnp.arange(block_rows, dtype=jnp.int32)
    same = (owners[:, None] == owners[None, :]) & wanted[:, None] & wanted[None, :]
    rank = jnp.sum((same & (order[None, :] < order[:, None])).astype(jnp.int32), axis=1)
    mine = jnp.sum(
        jnp.where(jnp.arange(owner_count) == my_index, extra.reshape(owner_count, owner_count), 0), axis=1
    ).reshape(2, planes, 2)
    mine = flip(flip(mine, 0, my_x), 2, my_core).transpose(1, 0, 2).reshape(planes, 4)
    begin = exclusive(mine, 1).reshape(planes, 2, 2).transpose(1, 0, 2)
    begin = flip(flip(begin, 0, my_x), 2, my_core).reshape(owner_count)
    owner_hit = owners[:, None] == jnp.arange(owner_count, dtype=jnp.int32)[None, :]
    begin = jnp.sum(jnp.where(owner_hit, begin[None, :], 0), axis=1)
    is_direct = rank < DIRECT
    direct_at = owners * DIRECT + rank
    plane_of = (owners // 2) % planes
    plane_at = begin + rank - DIRECT
    prefix_count = req_count * prefix_pages
    shape = (req_count, prefix_pages)
    prefix_direct = (is_direct & wanted)[:prefix_count].reshape(shape)
    first_lists = page_lists(prefix_direct, direct_at[:prefix_count].reshape(shape), seen)

    decay_sum = jnp.cumsum(step_sizes * decay_rates[None, None, :], axis=1)
    ds_cols = decay_sum.reshape(req_count, new_count, groups, GROUP_HEADS).transpose(0, 2, 1, 3)
    ds_rows = ds_cols.transpose(0, 1, 3, 2)
    dt_rows = step_sizes.reshape(req_count, new_count, groups, GROUP_HEADS).transpose(0, 2, 3, 1)
    skip_cols = jnp.repeat(skip_weights, HEAD_P).reshape(1, 1, width)
    fresh = fresh_part(ssm_values, ssm_keys, ssm_queries, ds_cols, ds_rows, dt_rows, skip_cols)
    acc, top = attend_new(att_queries, new_keyvals)

    acc_1, top_1 = attend_paged(
        False, *first_lists, new_lengths, late_queries, acc, top, (arrived,)
    )

    def late_pages(size):
        def run():
            rows = late_rows[:, :size].reshape(-1)
            going = pick(rows, page_pool, from_core, from_cross, cross_more)
            late = lax.all_to_all(
                going.reshape((planes, size) + page_shape), "z", 0, 0, tiled=True
            )
            late = jnp.pad(late, ((0, 0), (0, LATE_ROWS - size), (0, 0), (0, 0)))
            return late.reshape((planes * LATE_ROWS,) + page_shape)

        return run

    def no_pages():
        return jnp.zeros((planes * LATE_ROWS,) + page_shape, page_pool.dtype)

    choice = (most > READY_ROWS).astype(jnp.int32) + (most > READY_ROWS + 1).astype(jnp.int32)
    come_late = lax.switch(choice, [no_pages, late_pages(1), late_pages(LATE_ROWS)])

    late_at = jnp.where(
        plane_at < READY_ROWS,
        plane_of * READY_ROWS + plane_at,
        planes * READY_ROWS + plane_of * LATE_ROWS + plane_at - READY_ROWS,
    )
    late = (wanted & ~is_direct)[:prefix_count].reshape(shape)
    last_lists = page_lists(late, late_at[:prefix_count].reshape(shape), seen)
    landed = jnp.where(is_direct, direct_at, owner_count * DIRECT + late_at)
    attention = attend_paged(
        True, *last_lists, new_lengths, att_queries, acc_1, top_1, (come, come_late)
    )
    mixer = mixer_part(
        landed[prefix_count:],
        new_lengths,
        fresh,
        ssm_gate,
        ssm_queries,
        ds_cols,
        norm_gain.reshape(1, 1, width),
        (arrived, come, come_late),
    )
    return mixer, attention


def solution(mesh):
    devices = mesh.devices
    split = Mesh(
        devices.reshape(2, devices.shape[0] // 4, 2, devices.shape[1]), BATCH + ("head",)
    )
    return jax.shard_map(
        body,
        mesh=split,
        in_specs=(
            P(BATCH, None, "head"),
            P(BATCH, None, "head"),
            P(BATCH, None, "head"),
            P(BATCH, None, "head"),
            P(BATCH, None, "head"),
            P("head"),
            P("head"),
            P("head"),
            P(BATCH, None, "head"),
            P(BATCH, None, "head"),
            P(BATCH, "head", None),
            P(BATCH, None, None),
            P(BATCH, None),
            P(BATCH),
            P(BATCH),
        ),
        out_specs=(P(BATCH, None, "head"), P(BATCH, None, "head")),
        check_vma=False,
    )
```
